32 devices in a mesh: groups: 2 (over x), ctx: 16 (over z, y, core).
Axes of the slice: x: 2, y: 2, z: 4, core: 2. Of those that a mesh axis runs over, the one named last changes fastest.
Arguments:
- queries: bfloat16 [8192, 1152], P(('groups', 'ctx')), parts along dimension 0, may hold values from -40 to 40
- keys: bfloat16 [8192, 1152], P(('groups', 'ctx')), parts along dimension 0, may hold values from -40 to 40
- values: bfloat16 [8192, 1152], P(('groups', 'ctx')), parts along dimension 0, may hold values from -6 to 6
- upstream: bfloat16 [8192, 1152], P(('groups', 'ctx')), parts along dimension 0, may hold values from -6 to 6
- lengths: int32 [12], P('groups'), parts along dimension 0, may hold values from 1 to 2, 8 in all
- modality: int32 [12], P('groups'), parts along dimension 0, may hold values from 0 to 1
- pairs: int32 [12], P('groups'), parts along dimension 0, may hold values from 0 to 5, as said below
- texts: float32 [12, 1152], P('groups'), parts along dimension 0, may hold values from -6 to 6
- modality_bias: float32 [2], replicated, may hold values from -12 to -4
Outputs:
- grad_queries: bfloat16 [8192, 1152], P(('groups', 'ctx')), parts along dimension 0
- grad_keys: bfloat16 [8192, 1152], P(('groups', 'ctx')), parts along dimension 0
- grad_values: bfloat16 [8192, 1152], P(('groups', 'ctx')), parts along dimension 0
- loss: float32 [12], P('groups'), parts along dimension 0
The draws below stay inside these ranges and needn't reach their ends.
There are 2 independent parts, one for each index of `groups`. The reference program is written for one: setup_inputs(seed, part) draws one part's arguments, and reference() takes and returns one part's arrays. A program takes and returns all parts, laid end to end along the dimension named above; an argument that names none is the same for every part. Nothing has to cross between parts.
Inputs may be any that keep to these rules, and one draw needn't show every extreme that they name: `lengths`: the blocks of all scenes add up to 8, and some scene has 2 blocks. `pairs`: each caption belongs to exactly one scene.
All inputs are finite; a program needn't handle non-finite values.
Results may differ from the reference program's by a relative error of at most 0.0024.
The reference program's roundings to bfloat16 on the way count: a program that leaves them out, or rounds other values in their place, can miss the bound.
Values may be sent and summed in bfloat16 or wider, within the bound.
A program may use at most 128 MiB of HBM per device.

```python
import math
import jax
import jax.numpy as jnp
import numpy as np
from jax import lax

HEADS = 16
HEAD_DIM = 72
D = 1152
BLOCK = 512
MAXB = 2
TOKENS = 4096
BLOCKS = 8
SCENES = 6


def draw_queries(key, part):
    key = jax.random.fold_in(key, 11)
    own = jnp.clip(jax.random.normal(key, (TOKENS, D), jnp.float32), -6.0, 6.0)
    return own.astype(jnp.bfloat16)


def draw_keys(key, part):
    key = jax.random.fold_in(key, 12)
    own = jnp.clip(jax.random.normal(key, (TOKENS, D), jnp.float32), -6.0, 6.0)
    return own.astype(jnp.bfloat16)


def draw_pairs(key, part):
    key = jax.random.fold_in(key, 13)
    return jax.random.permutation(key, SCENES).astype(jnp.int32)


def plant(entries, key, smallest, top_value):
    dims = entries.shape
    spot = [jax.random.randint(jax.random.fold_in(key, axis), (), 0, dims[axis]) for axis in range(len(dims))]
    entries = entries.at[tuple(spot)].set(smallest)
    longest = dims.index(max(dims))
    spot[longest] = (spot[longest] + 1) % dims[longest]
    return entries.at[tuple(spot)].set(top_value)


def levels(own_key, extent, shards, low, largest):
    factor_of = 1.0
    for position, blocks in shards:
        draws = jax.random.uniform(jax.random.fold_in(jax.random.fold_in(own_key, 6), position), (blocks,), jnp.float32, low / len(shards), largest / len(shards))
        factor_of = factor_of * jnp.repeat(jnp.exp(draws), extent[position] // blocks).reshape((-1,) + (1,) * (len(extent) - 1 - position))
    return factor_of


def length_profile(count, total, limit, lean):
    weights = [(1 << 20) // math.isqrt(rank ** lean) + 1 for rank in range(2, count + 1)]
    rest, holding = total - limit - (count - 1), [1] * (count - 1)
    while rest > 0:
        movable = [i for i in range(count - 1) if holding[i] < limit]
        mass, left = sum([weights[i] for i in movable]), rest
        for i in movable:
            more = min(limit - holding[i], max(1, left * weights[i] // mass), rest)
            holding[i] = holding[i] + more
            rest = rest - more
    return np.array([limit] + holding)


def ragged(key, count, total, most, lean):
    if count == 2:
        one = jax.random.randint(key, (), max(1, total - most), min(most, total - 1) + 1)
        return jnp.stack([one, total - one])
    sizes = jnp.asarray(length_profile(count, total, most, lean), jnp.int32)
    twos = (count - 1) // 2
    source_of, receiver = sizes[1:1 + 2 * twos:2], sizes[2:2 + 2 * twos:2]
    slack = jnp.minimum(source_of - 1, most - receiver)
    moved = jax.random.randint(jax.random.fold_in(key, 1), (twos,), 0, 1 << 20) % (slack + 1)
    sizes = sizes.at[1:1 + 2 * twos:2].set(source_of - moved).at[2:2 + 2 * twos:2].set(receiver + moved)
    return sizes[jax.random.permutation(jax.random.fold_in(key, 2), count)]


def scatter_about(key, dims, spread, bound, shards=(), kind=jnp.bfloat16):
    drawn = jax.random.normal(key, dims, jnp.float32) * spread
    if len(shards) > 0:
        drawn = levels(key, dims, shards, -0.22, 0.18) * drawn
    return jnp.clip(drawn, min=-bound, max=bound).astype(kind)


def setup_inputs(seed: int = 0, part: int = 0) -> dict:
    key_of = jax.random.split(jax.random.key(seed), 10)
    own_keys = jax.random.split(jax.random.fold_in(key_of[9], part), 10)
    queries = draw_queries(jax.random.fold_in(jax.random.fold_in(key_of[9], part), 71), part)
    keys = draw_keys(jax.random.fold_in(jax.random.fold_in(key_of[9], part), 71), part)
    values = scatter_about(own_keys[2], (TOKENS, D), 1.0, 6.0, ((0, 16),))
    upstream = scatter_about(own_keys[3], (TOKENS, D), 1.0, 6.0, ((0, 16),))
    lengths = ragged(own_keys[4], SCENES, BLOCKS, MAXB, 0).astype(jnp.int32)
    modality = plant(jax.random.randint(own_keys[5], (SCENES,), 0, 2), jax.random.fold_in(own_keys[5], 1), 0, 1).astype(jnp.int32)
    pairs = draw_pairs(jax.random.fold_in(jax.random.fold_in(key_of[9], part), 71), part)
    texts = scatter_about(own_keys[7], (SCENES, D), 1.0, 6.0, (), jnp.float32)
    modality_bias = jnp.clip(jax.random.uniform(key_of[8], (2,), jnp.float32, -12.0, -4.0), -12.0, -4.0)
    return {"queries": queries, "keys": keys, "values": values, "upstream": upstream, "lengths": lengths, "modality": modality, "pairs": pairs, "texts": texts, "modality_bias": modality_bias}


TEMPER = 10.0
LOSS_SCALE = 65536.0
EPSILON = 1e-06

def scene_of(positions, lengths, total):
    ends = jnp.cumsum(lengths).astype(jnp.int32) * BLOCK
    found = lax.optimization_barrier(jnp.sum((positions[:, None] >= ends[None, :]).astype(jnp.int32), axis=1))
    inside = (positions >= 0) & (positions < total)
    return jnp.where(inside, found, -1).astype(jnp.int32)

def split_heads(x):
    return x.reshape(x.shape[0], HEADS, HEAD_DIM).transpose(1, 0, 2)

def join_heads(x):
    return x.transpose(1, 0, 2).reshape(x.shape[1], HEADS * HEAD_DIM)

def contrast(pooled_sum, lengths, modality, pairs, texts, modality_bias):
    count_rows = lengths.shape[0]
    sizes = (lengths * BLOCK).astype(jnp.float32)
    pooled = pooled_sum / sizes[:, None]
    norm = jnp.sqrt(lax.optimization_barrier(jnp.sum(pooled * pooled, axis=1, keepdims=True)) + EPSILON)
    unit = pooled / norm
    text_unit = texts / jnp.sqrt(lax.optimization_barrier(jnp.sum(texts * texts, axis=1, keepdims=True)) + EPSILON)
    bias = jnp.where(modality == 0, modality_bias[0], modality_bias[1])
    logits = TEMPER * jnp.dot(unit, text_unit.T, precision=lax.Precision.HIGHEST) + bias[:, None]
    labels = jnp.where(pairs[:, None] == jnp.arange(count_rows, dtype=jnp.int32)[None, :], 1.0, -1.0)
    margin = labels * logits
    loss = lax.optimization_barrier(jnp.sum(jax.nn.softplus(-margin), axis=1))
    grad_logits = -labels * jax.nn.sigmoid(-margin) * (LOSS_SCALE / count_rows)
    grad_unit = TEMPER * jnp.dot(grad_logits, text_unit, precision=lax.Precision.HIGHEST)
    grad_pooled = (grad_unit - unit * lax.optimization_barrier(jnp.sum(unit * grad_unit, axis=1, keepdims=True))) / norm
    return (loss, grad_pooled / sizes[:, None])

def reference(queries, keys, values, upstream, lengths, modality, pairs, texts, modality_bias):
    scale = HEAD_DIM ** (-0.5)
    margin_rows = (MAXB - 1) * BLOCK
    span = (2 * MAXB - 1) * BLOCK
    scene = scene_of(jnp.arange(TOKENS, dtype=jnp.int32), lengths, TOKENS)

    def widen(x, fill):
        pads = [(margin_rows, margin_rows)] + [(0, 0)] * (x.ndim - 1)
        return jnp.pad(x, pads, constant_values=fill)

    def middle(x, index):
        return lax.dynamic_slice_in_dim(x, index * BLOCK, BLOCK, 0)

    def beside_all(x, index):
        return lax.dynamic_slice_in_dim(x, index * BLOCK, span, 0)
    q_full = queries.astype(jnp.float32)
    k_full = keys.astype(jnp.float32)
    v_full = values.astype(jnp.float32)
    k_wide = widen(k_full, 0.0)
    v_wide = widen(v_full, 0.0)
    scene_wide = widen(scene, -1)

    def forward_block(index):
        q_heads = split_heads(middle(q_full, index))
        k_heads = split_heads(beside_all(k_wide, index))
        v_heads = split_heads(beside_all(v_wide, index))
        allowed = (middle(scene, index)[:, None] == beside_all(scene_wide, index)[None, :])[None]
        scores = jnp.einsum('hqd,hkd->hqk', q_heads, k_heads) * scale
        top = lax.optimization_barrier(jnp.max(jnp.where(allowed, scores, -jnp.inf), axis=2))
        total = lax.optimization_barrier(jnp.sum(jnp.where(allowed, jnp.exp(scores - top[:, :, None]), 0.0), axis=2))
        lse = top + jnp.log(total)
        probs = jnp.where(allowed, jnp.exp(scores - lse[:, :, None]), 0.0)
        probs = lax.optimization_barrier(probs.astype(jnp.bfloat16)).astype(jnp.float32)
        output = jnp.einsum('hqk,hkd->hqd', probs, v_heads)
        return (join_heads(output).astype(jnp.bfloat16), lse.T)
    block_ids = jnp.arange(TOKENS // BLOCK, dtype=jnp.int32)
    attended, lse_rows = lax.map(forward_block, block_ids)
    attended = attended.reshape(TOKENS, HEADS * HEAD_DIM)
    lse_rows = lse_rows.reshape(TOKENS, HEADS)
    member = (scene[None, :] == jnp.arange(SCENES, dtype=jnp.int32)[:, None]).astype(jnp.float32)
    pooled_sum = jnp.dot(member, attended.astype(jnp.float32), precision=lax.Precision.HIGHEST)
    loss, per_token = contrast(pooled_sum, lengths, modality, pairs, texts, modality_bias)
    grad_out = (upstream.astype(jnp.float32) + per_token[scene]).astype(jnp.bfloat16)
    g_full = grad_out.astype(jnp.float32)
    delta_rows = lax.optimization_barrier(jnp.sum(split_heads(g_full) * split_heads(attended.astype(jnp.float32)), axis=2)).T
    q_wide = widen(q_full, 0.0)
    g_wide = widen(g_full, 0.0)
    lse_wide = widen(lse_rows, 0.0)
    delta_wide = widen(delta_rows, 0.0)

    def query_block(index):
        q_heads = split_heads(middle(q_full, index))
        g_heads = split_heads(middle(g_full, index))
        lse = middle(lse_rows, index).T
        delta = middle(delta_rows, index).T
        k_heads = split_heads(beside_all(k_wide, index))
        v_heads = split_heads(beside_all(v_wide, index))
        allowed = (middle(scene, index)[:, None] == beside_all(scene_wide, index)[None, :])[None]
        scores = jnp.einsum('hqd,hkd->hqk', q_heads, k_heads) * scale
        probs = jnp.where(allowed, jnp.exp(scores - lse[:, :, None]), 0.0)
        grad_probs = jnp.einsum('hqd,hkd->hqk', g_heads, v_heads)
        grad_scores = (probs * (grad_probs - delta[:, :, None])).astype(jnp.bfloat16)
        grad_scores = lax.optimization_barrier(grad_scores).astype(jnp.float32)
        grad_q = jnp.einsum('hqk,hkd->hqd', grad_scores, k_heads) * scale
        return join_heads(grad_q).astype(jnp.bfloat16)

    def key_block(index):
        k_heads = split_heads(middle(k_full, index))
        v_heads = split_heads(middle(v_full, index))
        q_heads = split_heads(beside_all(q_wide, index))
        g_heads = split_heads(beside_all(g_wide, index))
        lse = beside_all(lse_wide, index).T
        delta = beside_all(delta_wide, index).T
        allowed = (beside_all(scene_wide, index)[:, None] == middle(scene, index)[None, :])[None]
        scores = jnp.einsum('hqd,hkd->hqk', q_heads, k_heads) * scale
        probs = jnp.where(allowed, jnp.exp(scores - lse[:, :, None]), 0.0)
        grad_probs = jnp.einsum('hqd,hkd->hqk', g_heads, v_heads)
        grad_scores = (probs * (grad_probs - delta[:, :, None])).astype(jnp.bfloat16)
        grad_scores = lax.optimization_barrier(grad_scores).astype(jnp.float32)
        rounded = lax.optimization_barrier(probs.astype(jnp.bfloat16)).astype(jnp.float32)
        grad_k = jnp.einsum('hqk,hqd->hkd', grad_scores, q_heads) * scale
        grad_v = jnp.einsum('hqk,hqd->hkd', rounded, g_heads)
        return (join_heads(grad_k).astype(jnp.bfloat16), join_heads(grad_v).astype(jnp.bfloat16))
    grad_queries = lax.map(query_block, block_ids).reshape(TOKENS, HEADS * HEAD_DIM)
    grad_keys, grad_values = lax.map(key_block, block_ids)
    grad_keys = grad_keys.reshape(TOKENS, HEADS * HEAD_DIM)
    grad_values = grad_values.reshape(TOKENS, HEADS * HEAD_DIM)
    return (grad_queries, grad_keys, grad_values, loss)
```

```python
import jax
import jax.numpy as jnp
from jax import lax
from jax.experimental import pallas as pl
from jax.experimental.pallas import tpu as pltpu
from jax.sharding import PartitionSpec as P

HEADS = 16
HEAD_DIM = 72
BLOCK = 512
QUARTER = 4
CHUNK = 256
TEMPER = 10.0
LOSS_SCALE = 65536.0
EPSILON = 1e-06
SCALE = HEAD_DIM ** (-0.5)
LOG2E = 1.4426950408889634
FAR = -1e30


def dot_over(x, y, dim_x, dim_y):
    return lax.dot_general(
        x, y, (((dim_x,), (dim_y,)), ((), ())), preferred_element_type=jnp.float32
    )


def attend_kernel(far_ref, a_ref, b_ref, att_a, att_b, lse_a, lse_b, pool_ref):
    far = far_ref[0]
    sides = (a_ref, b_ref)
    lane = lax.broadcasted_iota(jnp.int32, (HEAD_DIM, 128), 1)
    pools = []
    for own in range(2):
        pool = jnp.zeros((HEAD_DIM, 1), jnp.float32)
        for start in range(0, BLOCK, CHUNK):
            q = sides[own][0, 0, :, start : start + CHUNK]
            scores = []
            for side in range(2):
                s = dot_over(sides[side][1, 0], q, 0, 0) * (SCALE * LOG2E)
                scores.append(s if side == own else s + far)
            top = jnp.maximum(
                jnp.max(scores[0], axis=0, keepdims=True),
                jnp.max(scores[1], axis=0, keepdims=True),
            )
            parts = [jnp.exp2(s - top) for s in scores]
            total = jnp.sum(parts[0], axis=0, keepdims=True) + jnp.sum(
                parts[1], axis=0, keepdims=True
            )
            scale = 1.0 / total
            att = jnp.zeros((HEAD_DIM, CHUNK), jnp.float32)
            for side in range(2):
                probs = (parts[side] * scale).astype(jnp.bfloat16)
                att = att + dot_over(sides[side][2, 0], probs, 1, 0)
            att = att.astype(jnp.bfloat16)
            (att_a, att_b)[own][0, :, start : start + CHUNK] = att
            (lse_a, lse_b)[own][0, :, start : start + CHUNK] = top + jnp.log2(total)
            pool = pool + jnp.sum(att.astype(jnp.float32), axis=1, keepdims=True)
        pools.append(pool)
    pool_ref[0] = jnp.where(lane == 0, pools[0], jnp.where(lane == 1, pools[1], 0.0))


def grads_kernel(
    far_ref, a_ref, b_ref, ua_ref, ub_ref, att_a, att_b, lse_a, lse_b, ga_ref, gb_ref,
    out_a, out_b, acc_ref,
):
    far = far_ref[0]
    sides = (a_ref, b_ref)
    outs = (out_a, out_b)
    first = True
    for own in range(2):
        for start in range(0, BLOCK, CHUNK):
            span = slice(start, start + CHUNK)
            q = sides[own][0, 0, :, span]
            up = (ua_ref, ub_ref)[own][0, :, span].astype(jnp.float32)
            grad = (up + (ga_ref, gb_ref)[own][0]).astype(jnp.bfloat16)
            att = (att_a, att_b)[own][0, :, span].astype(jnp.float32)
            lse = (lse_a, lse_b)[own][0, :, span]
            delta = jnp.sum(grad.astype(jnp.float32) * att, axis=0, keepdims=True)
            grad_q = jnp.zeros((HEAD_DIM, CHUNK), jnp.float32)
            for side in range(2):
                k = sides[side][1, 0]
                s = dot_over(k, q, 0, 0) * (SCALE * LOG2E)
                if side != own:
                    s = s + far
                probs = jnp.exp2(s - lse)
                grad_probs = dot_over(sides[side][2, 0], grad, 0, 0)
                grad_scores = (probs * (grad_probs - delta)).astype(jnp.bfloat16)
                grad_q = grad_q + dot_over(k, grad_scores, 1, 0)
                grad_k = dot_over(q, grad_scores, 1, 1)
                grad_v = dot_over(grad, probs.astype(jnp.bfloat16), 1, 1)
                if first:
                    acc_ref[side, 0] = grad_k
                    acc_ref[side, 1] = grad_v
                else:
                    acc_ref[side, 0] += grad_k
                    acc_ref[side, 1] += grad_v
            first = False
            outs[own][0, 0, :, span] = (grad_q * SCALE).astype(jnp.bfloat16)
    for side in range(2):
        outs[side][1, 0] = (acc_ref[side, 0] * SCALE).astype(jnp.bfloat16)
        outs[side][2, 0] = acc_ref[side, 1].astype(jnp.bfloat16)


def head_block(lead, rows, columns):
    if lead:
        return pl.BlockSpec((lead, 1, rows, columns), lambda h: (0, h, 0, 0))
    return pl.BlockSpec((1, rows, columns), lambda h: (h, 0, 0))


SMEM = pl.BlockSpec(memory_space=pltpu.SMEM)


def attend(far, a, b):
    tile = jax.ShapeDtypeStruct((QUARTER, HEAD_DIM, BLOCK), jnp.bfloat16)
    line = jax.ShapeDtypeStruct((QUARTER, 1, BLOCK), jnp.float32)
    return pl.pallas_call(
        attend_kernel,
        grid=(QUARTER,),
        in_specs=[SMEM, head_block(3, HEAD_DIM, BLOCK), head_block(3, HEAD_DIM, BLOCK)],
        out_specs=[
            head_block(0, HEAD_DIM, BLOCK),
            head_block(0, HEAD_DIM, BLOCK),
            head_block(0, 1, BLOCK),
            head_block(0, 1, BLOCK),
            head_block(0, HEAD_DIM, 128),
        ],
        out_shape=[
            tile, tile, line, line,
            jax.ShapeDtypeStruct((QUARTER, HEAD_DIM, 128), jnp.float32),
        ],
        compiler_params=pltpu.CompilerParams(vmem_limit_bytes=48 * 2**20),
        cost_estimate=pl.CostEstimate(
            flops=4 * QUARTER * HEAD_DIM * 4 * BLOCK * BLOCK,
            bytes_accessed=5 * 10**6,
            transcendentals=QUARTER * 4 * BLOCK * BLOCK,
        ),
        name="attend",
    )(far, a, b)


def grads(far, a, b, ua, ub, att_a, att_b, lse_a, lse_b, ga, gb):
    tile = jax.ShapeDtypeStruct((3, QUARTER, HEAD_DIM, BLOCK), jnp.bfloat16)
    wide = head_block(3, HEAD_DIM, BLOCK)
    one = head_block(0, HEAD_DIM, BLOCK)
    line = head_block(0, 1, BLOCK)
    column = head_block(0, HEAD_DIM, 1)
    return pl.pallas_call(
        grads_kernel,
        grid=(QUARTER,),
        in_specs=[SMEM, wide, wide, one, one, one, one, line, line, column, column],
        out_specs=[wide, wide],
        out_shape=[tile, tile],
        scratch_shapes=[pltpu.VMEM((2, 2, HEAD_DIM, BLOCK), jnp.float32)],
        compiler_params=pltpu.CompilerParams(vmem_limit_bytes=48 * 2**20),
        cost_estimate=pl.CostEstimate(
            flops=10 * QUARTER * HEAD_DIM * 4 * BLOCK * BLOCK,
            bytes_accessed=8 * 10**6,
            transcendentals=QUARTER * 4 * BLOCK * BLOCK,
        ),
        name="grads",
    )(far, a, b, ua, ub, att_a, att_b, lse_a, lse_b, ga, gb)


def contrast_row(pooled_sum, size, kind, pair, texts, modality_bias, count):
    pooled = pooled_sum / size
    norm = jnp.sqrt(jnp.sum(pooled * pooled) + EPSILON)
    unit = pooled / norm
    text_unit = texts / jnp.sqrt(jnp.sum(texts * texts, axis=1, keepdims=True) + EPSILON)
    bias = jnp.where(kind == 0, modality_bias[0], modality_bias[1])
    logits = TEMPER * jnp.sum(text_unit * unit[None, :], axis=1) + bias
    labels = jnp.where(pair == jnp.arange(count, dtype=jnp.int32), 1.0, -1.0)
    margin = labels * logits
    loss = jnp.sum(jax.nn.softplus(-margin))
    grad_logits = -labels * jax.nn.sigmoid(-margin) * (LOSS_SCALE / count)
    grad_unit = TEMPER * jnp.sum(grad_logits[:, None] * text_unit, axis=0)
    grad_pooled = (grad_unit - unit * jnp.sum(unit * grad_unit)) / norm
    return loss, grad_pooled / size


def on_device(queries, keys, values, upstream, lengths, modality, pairs, texts, modality_bias):
    rows = queries.shape[0]
    devices = lax.axis_size("ctx")
    count = lengths.shape[0]
    place = lax.axis_index("ctx")
    block, core = place // 2, place % 2
    ends = jnp.cumsum(lengths)
    scene = jnp.sum((block >= ends).astype(jnp.int32))
    length = lengths[scene]
    second = block - (ends[scene] - length)
    paired = length == 2
    beside = (block - second + (1 - second)) == (block ^ 1)
    far = jnp.where(paired, 0.0, FAR).astype(jnp.float32).reshape(1)

    def swap_core(x):
        return lax.ppermute(x, "ctx", [(i, i ^ 1) for i in range(devices)])

    def across(x):
        return lax.ppermute(x, "ctx", [(i, i ^ 2) for i in range(devices)])

    def relayed(x):
        hops = [(i, i - 4 if i & 2 else i + 4) for i in range(devices)]
        hops = [(i, j) for i, j in hops if 0 <= j < devices]
        return lax.ppermute(x, "ctx", hops)

    def partner(x):
        near = across(x)
        return jnp.where(beside, near, relayed(near))

    def widened(x):
        x = x.T.reshape(2, 2, QUARTER, HEAD_DIM, rows)
        mine = lax.dynamic_index_in_dim(x, core, 1, keepdims=False)
        return mine, lax.dynamic_index_in_dim(x, 1 - core, 1, keepdims=False)

    def own_block(arrays):
        pieces = [widened(x) for x in arrays]
        mine = jnp.stack([p[0] for p in pieces])
        theirs = swap_core(jnp.stack([p[1] for p in pieces]))
        whole = jnp.concatenate([mine, theirs], axis=4)
        return (
            lax.dynamic_index_in_dim(whole, second, 1, keepdims=False),
            lax.dynamic_index_in_dim(whole, 1 - second, 1, keepdims=False),
        )

    a, given = own_block((queries, keys, values))
    ua, u_given = own_block((upstream,))
    b = jnp.where(paired, partner(given), given)
    ub = jnp.where(paired, partner(u_given), u_given)
    att_a, att_b, lse_a, lse_b, pool = attend(far, a, b)

    width = QUARTER * HEAD_DIM
    pool_a, pool_b = pool[:, :, 0].reshape(width), pool[:, :, 1].reshape(width)
    half_of_a = jnp.where(paired, second, 0)
    mine = jnp.where(paired, pool_a + pool_b, pool_a)
    halves = jnp.arange(2, dtype=jnp.int32)
    by_half = jnp.where(
        halves[:, None] == half_of_a, mine[None], jnp.where(paired, 0.0, pool_b[None])
    )
    sums = jnp.where(halves[None, :, None] == core, by_half[:, None, :], 0.0)
    sums = sums + swap_core(sums)
    from_before = lax.ppermute(sums, "ctx", [(i, i + 2) for i in range(devices - 2)])
    from_after = lax.ppermute(sums, "ctx", [(i + 2, i) for i in range(devices - 2)])
    sums = sums + jnp.where(paired, jnp.where(second == 1, from_before, from_after), 0.0)
    size = (length * BLOCK).astype(jnp.float32)
    loss_here, per_token = contrast_row(
        sums.reshape(-1), size, modality[scene], pairs[scene], texts, modality_bias, count
    )
    speaks = (core == 0) & (second == 0)
    loss = jnp.where((jnp.arange(count) == scene) & speaks, loss_here, 0.0)
    loss = lax.psum(loss, "ctx")
    per_half = lax.dynamic_index_in_dim(
        per_token.reshape(2, 2, QUARTER, HEAD_DIM, 1), core, 1, keepdims=False
    )
    ga = jnp.where(half_of_a == 1, per_half[1], per_half[0])
    gb = jnp.where(paired, ga, per_half[1])
    out_a, out_b = grads(far, a, b, ua[0], ub[0], att_a, att_b, lse_a, lse_b, ga, gb)

    back = partner(out_b)
    low = jnp.where(paired & (second == 1), back, out_a)
    high = jnp.where(paired, jnp.where(second == 1, out_a, back), out_b)
    whole = jnp.stack([low, high])
    mine = whole[..., :rows]
    theirs = swap_core(whole[..., rows:])
    even = jnp.where(core == 0, mine, theirs)
    odd = jnp.where(core == 0, theirs, mine)
    done = jnp.stack([even, odd], axis=1)
    done = done.transpose(2, 5, 0, 1, 3, 4).reshape(3, rows, HEADS * HEAD_DIM)
    return done[0], done[1], done[2], loss


def solution(mesh):
    tokens = P(("groups", "ctx"), None)
    in_specs = (
        tokens, tokens, tokens, tokens,
        P("groups"), P("groups"), P("groups"), P("groups", None), P(),
    )
    out_specs = (tokens, tokens, tokens, P("groups"))
    return jax.shard_map(
        on_device, mesh=mesh, in_specs=in_specs, out_specs=out_specs, check_vma=False
    )
```

```python
import jax
import jax.numpy as jnp
from jax import lax
from jax.experimental import pallas as pl
from jax.experimental.pallas import tpu as pltpu
from jax.sharding import PartitionSpec as P

HEADS = 16
HEAD_DIM = 72
BLOCK = 512
QUARTER = 4
CHUNK = 256
TEMPER = 10.0
LOSS_SCALE = 65536.0
EPSILON = 1e-06
SCALE = HEAD_DIM ** (-0.5)
LOG2E = 1.4426950408889634
FAR = -1e30


def dot_over(x, y, dim_x, dim_y):
    return lax.dot_general(
        x, y, (((dim_x,), (dim_y,)), ((), ())), preferred_element_type=jnp.float32
    )


def neighbours():
    devices = lax.axis_size("ctx")
    me = lax.axis_index("ctx")
    odd = (me // 2) % 2
    across = me + 2 - 4 * odd
    target = me + 4 - 8 * odd
    source = me - 4 + 8 * odd
    has_target = (target >= 0) & (target < devices)
    has_source = (source >= 0) & (source < devices)
    return across, target, source, has_target, has_source


def signal(barrier, device):
    pl.semaphore_signal(
        barrier, inc=1, device_id={"ctx": device}, device_id_type=pl.DeviceIdType.MESH
    )


def greet():
    across, target, source, has_target, has_source = neighbours()
    barrier = pltpu.get_barrier_semaphore()
    signal(barrier, across)
    pl.when(has_target)(lambda: signal(barrier, target))
    pl.when(has_source)(lambda: signal(barrier, source))
    peers = 1 + has_target.astype(jnp.int32) + has_source.astype(jnp.int32)
    pl.semaphore_wait(barrier, peers)


def hop(src, dst, sems, h, device):
    return pltpu.make_async_remote_copy(
        src_ref=src.at[h],
        dst_ref=dst.at[h],
        send_sem=sems.at[0, h],
        recv_sem=sems.at[1, h],
        device_id={"ctx": device},
        device_id_type=pl.DeviceIdType.MESH,
    )


def chosen(flag, x, y):
    return jnp.where(flag, x.astype(jnp.float32), y.astype(jnp.float32)).astype(jnp.bfloat16)


def attend_kernel(
    far_ref, flag_ref, a_ref, given_ref, b_ref, att_ref, lse_ref, pool_ref,
    near_ref, relay_ref, near_sems, relay_sems,
):
    across, target, _, has_target, has_source = neighbours()

    @pl.when(jnp.logical_not(has_source))
    def _():
        relay_ref[...] = jnp.zeros_like(relay_ref)

    greet()
    for h in range(QUARTER):
        hop(given_ref, near_ref, near_sems, h, across).start()

    def pass_on(h):
        hop(given_ref, near_ref, near_sems, h, across).wait_recv()
        pl.when(has_target)(lambda: hop(near_ref, relay_ref, relay_sems, h, target).start())

    pass_on(0)
    far = far_ref[0]
    paired = flag_ref[0] == 1
    beside = flag_ref[1] == 1
    lane = lax.broadcasted_iota(jnp.int32, (HEAD_DIM, 128), 1)

    def one_head(h, gathered):
        pl.when(h < QUARTER - 1)(lambda: pass_on(h + 1))
        pl.when(has_source)(
            lambda: hop(near_ref, relay_ref, relay_sems, h, target).wait_recv()
        )
        for kind in range(4):
            b_ref[h, kind] = chosen(
                paired,
                chosen(beside, near_ref[h, kind], relay_ref[h, kind]),
                given_ref[h, kind],
            )
        sides = (a_ref, b_ref)
        for own in range(2):
            pool = jnp.zeros((HEAD_DIM, 1), jnp.float32)
            for start in range(0, BLOCK, CHUNK):
                q = sides[own][h, 0, :, start : start + CHUNK]
                scores = []
                for side in range(2):
                    s = dot_over(sides[side][h, 1], q, 0, 0) * (SCALE * LOG2E)
                    scores.append(s if side == own else s + far)
                top = jnp.maximum(
                    jnp.max(scores[0], axis=0, keepdims=True),
                    jnp.max(scores[1], axis=0, keepdims=True),
                )
                parts = [jnp.exp2(s - top) for s in scores]
                total = jnp.sum(parts[0], axis=0, keepdims=True) + jnp.sum(
                    parts[1], axis=0, keepdims=True
                )
                scale = 1.0 / total
                att = jnp.zeros((HEAD_DIM, CHUNK), jnp.float32)
                for side in range(2):
                    probs = (parts[side] * scale).astype(jnp.bfloat16)
                    att = att + dot_over(sides[side][h, 2], probs, 1, 0)
                att = att.astype(jnp.bfloat16)
                att_ref[own, h, :, start : start + CHUNK] = att
                lse_ref[own, h, :, start : start + CHUNK] = top + jnp.log2(total)
                pool = pool + jnp.sum(att.astype(jnp.float32), axis=1, keepdims=True)
            gathered = jnp.where(lane == own * QUARTER + h, pool, gathered)
        return gathered

    pool_ref[...] = lax.fori_loop(
        0, QUARTER, one_head, jnp.zeros((HEAD_DIM, 128), jnp.float32)
    )
    for h in range(QUARTER):
        hop(given_ref, near_ref, near_sems, h, across).wait_send()

        @pl.when(has_target)
        def _():
            hop(near_ref, relay_ref, relay_sems, h, target).wait_send()


def grads_kernel(
    far_ref, flag_ref, a_ref, b_ref, att_ref, lse_ref, extra_ref, whole_ref,
    out_ref, near_ref, relay_ref, acc_ref, near_sems, relay_sems,
):
    across, target, _, has_target, has_source = neighbours()

    @pl.when(jnp.logical_not(has_source))
    def _():
        relay_ref[...] = jnp.zeros_like(relay_ref)

    greet()
    far = far_ref[0]
    paired = flag_ref[0] == 1
    beside = flag_ref[1] == 1
    late = flag_ref[2] == 1
    given_ref = out_ref.at[1]

    def pass_on(h):
        hop(given_ref, near_ref, near_sems, h, across).wait_recv()
        pl.when(has_target)(lambda: hop(near_ref, relay_ref, relay_sems, h, target).start())

    def one_head(h, carry):
        sides = (a_ref, b_ref)
        first = True
        for own in range(2):
            for start in range(0, BLOCK, CHUNK):
                span = slice(start, start + CHUNK)
                q = sides[own][h, 0, :, span]
                up = sides[own][h, 3, :, span].astype(jnp.float32)
                grad = (up + extra_ref[own, h]).astype(jnp.bfloat16)
                att = att_ref[own, h, :, span].astype(jnp.float32)
                lse = lse_ref[own, h, :, span]
                delta = jnp.sum(grad.astype(jnp.float32) * att, axis=0, keepdims=True)
                grad_q = jnp.zeros((HEAD_DIM, CHUNK), jnp.float32)
                for side in range(2):
                    k = sides[side][h, 1]
                    s = dot_over(k, q, 0, 0) * (SCALE * LOG2E)
                    if side != own:
                        s = s + far
                    probs = jnp.exp2(s - lse)
                    grad_probs = dot_over(sides[side][h, 2], grad, 0, 0)
                    grad_scores = (probs * (grad_probs - delta)).astype(jnp.bfloat16)
                    grad_q = grad_q + dot_over(k, grad_scores, 1, 0)
                    grad_k = dot_over(q, grad_scores, 1, 1)
                    grad_v = dot_over(grad, probs.astype(jnp.bfloat16), 1, 1)
                    if first:
                        acc_ref[side, 0] = grad_k
                        acc_ref[side, 1] = grad_v
                    else:
                        acc_ref[side, 0] += grad_k
                        acc_ref[side, 1] += grad_v
                first = False
                out_ref[own, h, 0, :, span] = (grad_q * SCALE).astype(jnp.bfloat16)
        for side in range(2):
            out_ref[side, h, 1] = (acc_ref[side, 0] * SCALE).astype(jnp.bfloat16)
            out_ref[side, h, 2] = acc_ref[side, 1].astype(jnp.bfloat16)
        hop(given_ref, near_ref, near_sems, h, across).start()
        pl.when(h > 0)(lambda: pass_on(h - 1))
        return carry

    lax.fori_loop(0, QUARTER, one_head, 0)
    pass_on(QUARTER - 1)

    def settle(h, carry):
        pl.when(has_source)(
            lambda: hop(near_ref, relay_ref, relay_sems, h, target).wait_recv()
        )
        for kind in range(3):
            mine, other = out_ref[0, h, kind], out_ref[1, h, kind]
            back = chosen(beside, near_ref[h, kind], relay_ref[h, kind])
            other = chosen(paired, back, other)
            whole_ref[0, h, kind] = chosen(late, other, mine)
            whole_ref[1, h, kind] = chosen(late, mine, other)
        return carry

    lax.fori_loop(0, QUARTER, settle, 0)
    for h in range(QUARTER):
        hop(given_ref, near_ref, near_sems, h, across).wait_send()

        @pl.when(has_target)
        def _():
            hop(near_ref, relay_ref, relay_sems, h, target).wait_send()


def gather_kernel(x_ref, out_ref, send_sem, recv_sem):
    devices = lax.axis_size("ctx")
    me = lax.axis_index("ctx")
    barrier = pltpu.get_barrier_semaphore()

    def peer(step):
        return (me + step) % devices

    def greet_one(step, carry):
        signal(barrier, peer(step))
        return carry

    lax.fori_loop(1, devices, greet_one, 0)
    pl.semaphore_wait(barrier, devices - 1)

    def copy(step, slot):
        return pltpu.make_async_remote_copy(
            src_ref=x_ref,
            dst_ref=out_ref.at[slot],
            send_sem=send_sem.at[step],
            recv_sem=recv_sem.at[step],
            device_id={"ctx": peer(step)},
            device_id_type=pl.DeviceIdType.MESH,
        )

    def send_one(step, carry):
        copy(step, me).start()
        return carry

    def wait_one(step, carry):
        done = copy(step, (me + devices - step) % devices)
        done.wait_recv()
        done.wait_send()
        return carry

    lax.fori_loop(1, devices, send_one, 0)
    out_ref[me] = x_ref[...]
    lax.fori_loop(1, devices, wait_one, 0)


SMEM = pl.BlockSpec(memory_space=pltpu.SMEM)
VMEM = pl.BlockSpec(memory_space=pltpu.VMEM)


def params(number):
    return pltpu.CompilerParams(
        vmem_limit_bytes=48 * 2**20, collective_id=number, has_side_effects=True
    )


def attend(far, flags, a, given):
    tiles = (QUARTER, 4, HEAD_DIM, BLOCK)
    sems = pltpu.SemaphoreType.DMA((2, QUARTER))
    return pl.pallas_call(
        attend_kernel,
        in_specs=[SMEM, SMEM, VMEM, VMEM],
        out_specs=[VMEM] * 4,
        out_shape=[
            jax.ShapeDtypeStruct(tiles, jnp.bfloat16),
            jax.ShapeDtypeStruct((2, QUARTER, HEAD_DIM, BLOCK), jnp.bfloat16),
            jax.ShapeDtypeStruct((2, QUARTER, 1, BLOCK), jnp.float32),
            jax.ShapeDtypeStruct((HEAD_DIM, 128), jnp.float32),
        ],
        scratch_shapes=[
            pltpu.VMEM(tiles, jnp.bfloat16), pltpu.VMEM(tiles, jnp.bfloat16), sems, sems,
        ],
        compiler_params=params(0),
        name="attend",
    )(far, flags, a, given)


def grads(far, flags, a, b, att, lse, extra):
    tiles = (QUARTER, 3, HEAD_DIM, BLOCK)
    sems = pltpu.SemaphoreType.DMA((2, QUARTER))
    return pl.pallas_call(
        grads_kernel,
        in_specs=[SMEM, SMEM] + [VMEM] * 5,
        out_specs=VMEM,
        out_shape=jax.ShapeDtypeStruct((2,) + tiles, jnp.bfloat16),
        scratch_shapes=[
            pltpu.VMEM((2,) + tiles, jnp.bfloat16),
            pltpu.VMEM(tiles, jnp.bfloat16),
            pltpu.VMEM(tiles, jnp.bfloat16),
            pltpu.VMEM((2, 2, HEAD_DIM, BLOCK), jnp.float32),
            sems, sems,
        ],
        compiler_params=params(1),
        name="grads",
    )(far, flags, a, b, att, lse, extra)


def gather(x):
    devices = lax.axis_size("ctx")
    return pl.pallas_call(
        gather_kernel,
        in_specs=[VMEM],
        out_specs=VMEM,
        out_shape=jax.ShapeDtypeStruct((devices,) + x.shape, x.dtype),
        scratch_shapes=[
            pltpu.SemaphoreType.DMA((devices,)), pltpu.SemaphoreType.DMA((devices,)),
        ],
        compiler_params=params(2),
        name="gather",
    )(x)


def contrast(pooled_sum, lengths, modality, pairs, texts, modality_bias):
    count_rows = lengths.shape[0]
    sizes = (lengths * BLOCK).astype(jnp.float32)
    pooled = pooled_sum / sizes[:, None]
    norm = jnp.sqrt(jnp.sum(pooled * pooled, axis=1, keepdims=True) + EPSILON)
    unit = pooled / norm
    text_unit = texts / jnp.sqrt(jnp.sum(texts * texts, axis=1, keepdims=True) + EPSILON)
    bias = jnp.where(modality == 0, modality_bias[0], modality_bias[1])
    logits = TEMPER * jnp.dot(unit, text_unit.T, precision=lax.Precision.HIGHEST) + bias[:, None]
    labels = jnp.where(
        pairs[:, None] == jnp.arange(count_rows, dtype=jnp.int32)[None, :], 1.0, -1.0
    )
    margin = labels * logits
    loss = jnp.sum(jax.nn.softplus(-margin), axis=1)
    grad_logits = -labels * jax.nn.sigmoid(-margin) * (LOSS_SCALE / count_rows)
    grad_unit = TEMPER * jnp.dot(grad_logits, text_unit, precision=lax.Precision.HIGHEST)
    grad_pooled = (grad_unit - unit * jnp.sum(unit * grad_unit, axis=1, keepdims=True)) / norm
    return (loss, grad_pooled / sizes[:, None])


def on_device(queries, keys, values, upstream, lengths, modality, pairs, texts, modality_bias):
    rows = queries.shape[0]
    devices = lax.axis_size("ctx")
    count = lengths.shape[0]
    blocks = devices // 2
    place = lax.axis_index("ctx")
    block, core = place // 2, place % 2
    ends = jnp.cumsum(lengths)
    every = jnp.arange(blocks, dtype=jnp.int32)
    scenes = jnp.sum((every[:, None] >= ends[None, :]).astype(jnp.int32), axis=1)
    lengths_at = lengths[scenes]
    paired_at = lengths_at == 2
    seconds = every - (ends[scenes] - lengths_at)
    scene, second, paired = scenes[block], seconds[block], paired_at[block]
    beside = (block + 1 - 2 * second) == (block ^ 1)
    far = jnp.where(paired, 0.0, FAR).astype(jnp.float32).reshape(1)
    flags = jnp.stack([paired, beside, second == 1]).astype(jnp.int32)

    def swap_core(x):
        return lax.ppermute(x, "ctx", [(i, i ^ 1) for i in range(devices)])

    split = jnp.stack(
        [
            x.T.reshape(2, 2, QUARTER, HEAD_DIM, rows)
            for x in (queries, keys, values, upstream)
        ],
        axis=3,
    )
    mine = lax.dynamic_index_in_dim(split, core, 1, keepdims=False)
    theirs = swap_core(lax.dynamic_index_in_dim(split, 1 - core, 1, keepdims=False))
    whole = jnp.concatenate([mine, theirs], axis=-1)
    a = lax.dynamic_index_in_dim(whole, second, 0, keepdims=False)
    given = lax.dynamic_index_in_dim(whole, 1 - second, 0, keepdims=False)
    b, att, lse, pool = attend(far, flags, a, given)

    message = jnp.pad(pool[:, : 2 * QUARTER].T, ((0, 0), (0, 128 - HEAD_DIM)))
    pools = gather(message)[:, :, :HEAD_DIM].reshape(blocks, 2, 2, QUARTER * HEAD_DIM)
    both = pools[:, :, 0] + pools[:, :, 1]
    halves = []
    for half in range(2):
        shared = jnp.where((seconds == half)[:, None, None], both, 0.0)
        halves.append(jnp.where(paired_at[:, None, None], shared, pools[:, :, half]))
    sums = jnp.stack(halves, axis=1).reshape(blocks, HEADS * HEAD_DIM)
    member = scenes[None, :] == jnp.arange(count, dtype=jnp.int32)[:, None]
    pooled_sum = jnp.sum(jnp.where(member[:, :, None], sums[None], 0.0), axis=1)
    loss, per_token = contrast(pooled_sum, lengths, modality, pairs, texts, modality_bias)
    per_half = lax.dynamic_index_in_dim(
        per_token[scene].reshape(2, 2, QUARTER, HEAD_DIM, 1), core, 1, keepdims=False
    )
    own = per_half[second]
    extra = jnp.stack([own, jnp.where(paired, own, per_half[1])])
    whole = grads(far, flags, a, b, att, lse, extra)
    theirs = swap_core(whole[..., rows:])
    mine = whole[..., :rows]
    even = jnp.where(core == 0, mine, theirs)
    odd = jnp.where(core == 0, theirs, mine)
    done = jnp.stack([even, odd], axis=1)
    done = done.transpose(3, 5, 0, 1, 2, 4).reshape(3, rows, HEADS * HEAD_DIM)
    return done[0], done[1], done[2], loss


def solution(mesh):
    tokens = P(("groups", "ctx"), None)
    in_specs = (
        tokens, tokens, tokens, tokens,
        P("groups"), P("groups"), P("groups"), P("groups", None), P(),
    )
    out_specs = (tokens, tokens, tokens, P("groups"))
    return jax.shard_map(
        on_device, mesh=mesh, in_specs=in_specs, out_specs=out_specs, check_vma=False
    )
```

```python
import jax
import jax.numpy as jnp
from jax import lax
from jax.experimental import pallas as pl
from jax.experimental.pallas import tpu as pltpu
from jax.sharding import PartitionSpec as P

HEADS = 16
HEAD_DIM = 72
BLOCK = 512
QUARTER = 4
CHUNK = 256
TEMPER = 10.0
LOSS_SCALE = 65536.0
EPSILON = 1e-06
SCALE = HEAD_DIM ** (-0.5)
LOG2E = 1.4426950408889634
FAR = -1e30


def dot_over(x, y, dim_x, dim_y):
    return lax.dot_general(
        x, y, (((dim_x,), (dim_y,)), ((), ())), preferred_element_type=jnp.float32
    )


def chosen(flag, x, y):
    return jnp.where(flag, x.astype(jnp.float32), y.astype(jnp.float32)).astype(jnp.bfloat16)


def step_kernel(
    lengths_ref, modality_ref, pairs_ref, bias_ref,
    q_ref, k_ref, v_ref, u_ref, texts_ref,
    gq_ref, gk_ref, gv_ref, loss_ref,
    send_ref, sendu_ref, near_ref, nearu_ref, relay_ref, relayu_ref, swap_ref,
    a_ref, b_ref, att_ref, lse_ref, note_ref, pools_ref, extra_ref,
    res_ref, back_ref, far_back_ref, swap_back_ref, acc_ref,
    swap_sems, near_sems, relay_sems, note_sems, back_sems, far_back_sems, swap_back_sems,
):
    devices = lax.axis_size("ctx")
    blocks = devices // 2
    count = texts_ref.shape[0]
    rows = BLOCK // 2
    me = lax.axis_index("ctx")
    core = me % 2
    block = me // 2
    odd = block % 2
    mate = me + 1 - 2 * core
    across = (block + 1 - 2 * odd) * 2
    target = me + 4 - 8 * odd
    source = me - 4 + 8 * odd
    has_target = (target >= 0) & (target < devices)
    has_source = (source >= 0) & (source < devices)

    barrier = pltpu.get_barrier_semaphore()

    def peer(step):
        return (me + step) % devices

    def greet_one(step, carry):
        pl.semaphore_signal(
            barrier, inc=1, device_id={"ctx": peer(step)}, device_id_type=pl.DeviceIdType.MESH
        )
        return carry

    lax.fori_loop(1, devices, greet_one, 0)

    def place_of(at):
        scene, start, length, end = 0, 0, 0, 0
        for s in range(count):
            begin = end
            end = end + lengths_ref[s]
            here = (at >= begin) & (at < end)
            scene = jnp.where(here, s, scene)
            start = jnp.where(here, begin, start)
            length = jnp.where(here, lengths_ref[s], length)
        return scene, at - start, length

    scene, second, length = place_of(block)
    paired = length == 2
    late = second == 1
    beside = (block + 1 - 2 * second) == (block + 1 - 2 * odd)
    far = jnp.where(paired, 0.0, FAR).astype(jnp.float32)
    inputs = (q_ref, k_ref, v_ref, u_ref)

    def remote(src, dst, send_sem, recv_sem, device):
        return pltpu.make_async_remote_copy(
            src_ref=src,
            dst_ref=dst,
            send_sem=send_sem,
            recv_sem=recv_sem,
            device_id={"ctx": device},
            device_id_type=pl.DeviceIdType.MESH,
        )

    def swap(kind):
        return remote(
            inputs[kind].at[:, 1 - core], swap_ref.at[kind],
            swap_sems.at[0, kind], swap_sems.at[1, kind], mate,
        )

    def near(h, to, slot):
        return remote(
            send_ref.at[to, h], near_ref.at[slot, h],
            near_sems.at[0, to, h], near_sems.at[1, slot, h], across + to,
        )

    def near_up(to, slot):
        return remote(
            sendu_ref.at[to], nearu_ref.at[slot],
            near_sems.at[0, to, QUARTER], near_sems.at[1, slot, QUARTER], across + to,
        )

    def relay(h, slot):
        return remote(
            near_ref.at[slot, h], relay_ref.at[slot, h],
            relay_sems.at[0, slot, h], relay_sems.at[1, slot, h], target,
        )

    def relay_up(slot):
        return remote(
            nearu_ref.at[slot], relayu_ref.at[slot],
            relay_sems.at[0, slot, QUARTER], relay_sems.at[1, slot, QUARTER], target,
        )

    def back(h, to, slot):
        return remote(
            res_ref.at[1, to, h], back_ref.at[slot, h],
            back_sems.at[0, to, h], back_sems.at[1, slot, h], across + to,
        )

    def far_back(h, slot):
        return remote(
            back_ref.at[slot, h], far_back_ref.at[slot, h],
            far_back_sems.at[0, slot, h], far_back_sems.at[1, slot, h], target,
        )

    def swap_back(h, side):
        return remote(
            res_ref.at[side, 1, h], swap_back_ref.at[side, h],
            swap_back_sems.at[0, side, h], swap_back_sems.at[1, side, h], mate,
        )

    @pl.when(jnp.logical_not(has_source))
    def _():
        relay_ref[...] = jnp.zeros_like(relay_ref)
        relayu_ref[...] = jnp.zeros_like(relayu_ref)
        far_back_ref[...] = jnp.zeros_like(far_back_ref)

    def fill(h, carry):
        for to in range(2):
            for kind in range(3):
                send_ref[to, h, kind] = chosen(
                    late, inputs[kind][0, to, h], inputs[kind][1, to, h]
                )
            sendu_ref[to, h] = chosen(late, u_ref[0, to, h], u_ref[1, to, h])
        return carry

    lax.fori_loop(0, QUARTER, fill, 0)
    pl.semaphore_wait(barrier, devices - 1)
    for h in range(QUARTER):
        for to in range(2):
            near(h, to, core).start()
        swap(h).start()
    for to in range(2):
        near_up(to, core).start()

    def pass_on(h):
        for slot in range(2):
            near(h, slot, slot).wait_recv()
        for slot in range(2):
            pl.when(has_target)(lambda slot=slot: relay(h, slot).start())

    for kind in range(4):
        swap(kind).wait_recv()
    pass_on(0)
    lane = lax.broadcasted_iota(jnp.int32, (HEAD_DIM, 128), 1)
    sides = (a_ref, b_ref)

    def own_tiles(h, kind, near_pair, relay_pair):
        x = inputs[kind]
        low, high = x[0, core, h], x[1, core, h]
        low_far, high_far = swap_ref[kind, 0, h], swap_ref[kind, 1, h]
        a_ref[h, kind, :, :rows] = chosen(late, high, low)
        a_ref[h, kind, :, rows:] = chosen(late, high_far, low_far)
        for slot, alone in ((0, high), (1, high_far)):
            b_ref[h, kind, :, slot * rows : (slot + 1) * rows] = chosen(
                paired, chosen(beside, near_pair[slot], relay_pair[slot]), alone
            )

    def one_head(h, gathered):
        pl.when(h < QUARTER - 1)(lambda: pass_on(h + 1))

        @pl.when(has_source)
        def _():
            for slot in range(2):
                relay(h, slot).wait_recv()

        for kind in range(3):
            own_tiles(
                h, kind,
                [near_ref[slot, h, kind] for slot in range(2)],
                [relay_ref[slot, h, kind] for slot in range(2)],
            )
        for own in range(2):
            pool = jnp.zeros((HEAD_DIM, 1), jnp.float32)
            for start in range(0, BLOCK, CHUNK):
                q = sides[own][h, 0, :, start : start + CHUNK]
                scores = []
                for side in range(2):
                    s = dot_over(sides[side][h, 1], q, 0, 0) * (SCALE * LOG2E)
                    scores.append(s if side == own else s + far)
                top = jnp.maximum(
                    jnp.max(scores[0], axis=0, keepdims=True),
                    jnp.max(scores[1], axis=0, keepdims=True),
                )
                parts = [jnp.exp2(s - top) for s in scores]
                total = jnp.sum(parts[0], axis=0, keepdims=True) + jnp.sum(
                    parts[1], axis=0, keepdims=True
                )
                scale = 1.0 / total
                att = jnp.zeros((HEAD_DIM, CHUNK), jnp.float32)
                for side in range(2):
                    probs = (parts[side] * scale).astype(jnp.bfloat16)
                    att = att + dot_over(sides[side][h, 2], probs, 1, 0)
                att = att.astype(jnp.bfloat16)
                att_ref[own, h, :, start : start + CHUNK] = att
                lse_ref[own, h, :, start : start + CHUNK] = top + jnp.log2(total)
                pool = pool + jnp.sum(att.astype(jnp.float32), axis=1, keepdims=True)
            gathered = jnp.where(lane == own * QUARTER + h, pool, gathered)
        return gathered

    pool = lax.fori_loop(0, QUARTER, one_head, jnp.zeros((HEAD_DIM, 128), jnp.float32))
    pool = jnp.concatenate([pool, jnp.zeros((128 - HEAD_DIM, 128), jnp.float32)], axis=0)
    note_ref[...] = pool.T[: 2 * QUARTER]

    def note(step, slot):
        return remote(
            note_ref, pools_ref.at[slot], note_sems.at[0, step], note_sems.at[1, step], peer(step)
        )

    def send_note(step, carry):
        note(step, me).start()
        return carry

    lax.fori_loop(1, devices, send_note, 0)
    pools_ref[me] = note_ref[...]
    for slot in range(2):
        near_up(slot, slot).wait_recv()
    for slot in range(2):
        pl.when(has_target)(lambda slot=slot: relay_up(slot).start())

    text = texts_ref[...]

    def total_of(x):
        return jnp.sum(jnp.sum(x, axis=2, keepdims=True), axis=1, keepdims=True)

    text_unit = text / jnp.sqrt(total_of(text * text) + EPSILON)
    which = lax.broadcasted_iota(jnp.int32, (count, 1, 1), 0)
    which_full = lax.broadcasted_iota(jnp.int32, (count, 16, 128), 0)
    row_half = lax.broadcasted_iota(jnp.int32, (8, 128), 0) // QUARTER

    def wait_note(step, carry):
        done = note(step, (me + devices - step) % devices)
        done.wait_recv()
        done.wait_send()
        return carry

    lax.fori_loop(1, devices, wait_note, 0)

    def add_block(at, sums):
        its_scene, its_second, its_length = place_of(at)
        pieces = []
        for its_core in range(2):
            x = pools_ref[2 * at + its_core]
            both = x + jnp.concatenate([x[QUARTER:], x[:QUARTER]], axis=0)
            both = jnp.where(row_half == its_second, both, 0.0)
            pieces.append(jnp.where(its_length == 2, both, x))
        piece = jnp.concatenate(pieces, axis=0)
        return sums + jnp.where(which_full == its_scene, piece[None], 0.0)

    sums = lax.fori_loop(0, blocks, add_block, jnp.zeros((count, 16, 128), jnp.float32))
    sizes = jnp.zeros((count, 1, 1), jnp.float32)
    for s in range(count):
        sizes = jnp.where(which == s, (lengths_ref[s] * BLOCK).astype(jnp.float32), sizes)
    pooled = sums / sizes
    norm = jnp.sqrt(total_of(pooled * pooled) + EPSILON)
    unit = pooled / norm
    loss = jnp.zeros((8, 128), jnp.float32)
    loss_lane = lax.broadcasted_iota(jnp.int32, (8, 128), 1)
    grad_logits = jnp.zeros((count, 1, 1), jnp.float32)
    for i in range(count):
        bias = jnp.where(modality_ref[i] == 0, bias_ref[0], bias_ref[1])
        logits = TEMPER * total_of(text_unit * unit[i : i + 1]) + bias
        label = jnp.where(which == pairs_ref[i], 1.0, -1.0)
        margin = label * logits
        plus = jnp.maximum(-margin, 0.0) + jnp.log1p(jnp.exp(-jnp.abs(margin)))
        loss = jnp.where(loss_lane == i, jnp.sum(plus, axis=0), loss)
        slope = -label / (1.0 + jnp.exp(margin)) * (LOSS_SCALE / count)
        grad_logits = jnp.where(scene == i, slope, grad_logits)
    loss_ref[...] = loss
    grad_unit = TEMPER * jnp.sum(grad_logits * text_unit, axis=0, keepdims=True)
    mine = which == scene
    my_unit = jnp.sum(jnp.where(which_full == scene, unit, 0.0), axis=0, keepdims=True)
    my_norm = jnp.sum(jnp.where(mine, norm, 0.0), axis=0, keepdims=True)
    my_size = (length * BLOCK).astype(jnp.float32)
    grad_pooled = (grad_unit - my_unit * total_of(my_unit * grad_unit)) / my_norm
    per_token = (grad_pooled / my_size)[0]
    per_core = jnp.where(core == 0, per_token[:8], per_token[8:])
    columns = jnp.concatenate([per_core, jnp.zeros((120, 128), jnp.float32)], axis=0).T
    for h in range(QUARTER):
        low = columns[:HEAD_DIM, h : h + 1]
        high = columns[:HEAD_DIM, QUARTER + h : QUARTER + h + 1]
        own = jnp.where(late, high, low)
        extra_ref[0, h] = own
        extra_ref[1, h] = jnp.where(paired, own, high)

    @pl.when(has_source)
    def _():
        for slot in range(2):
            relay_up(slot).wait_recv()

    def pass_back(h):
        for slot in range(2):
            back(h, slot, slot).wait_recv()
        for slot in range(2):
            pl.when(has_target)(lambda slot=slot: far_back(h, slot).start())

    def one_grad(h, carry):
        own_tiles(
            h, 3,
            [nearu_ref[slot, h] for slot in range(2)],
            [relayu_ref[slot, h] for slot in range(2)],
        )
        first = True
        for own in range(2):
            for start in range(0, BLOCK, CHUNK):
                span = slice(start, start + CHUNK)
                q = sides[own][h, 0, :, span]
                up = sides[own][h, 3, :, span].astype(jnp.float32)
                grad = (up + extra_ref[own, h]).astype(jnp.bfloat16)
                att = att_ref[own, h, :, span].astype(jnp.float32)
                lse = lse_ref[own, h, :, span]
                delta = jnp.sum(grad.astype(jnp.float32) * att, axis=0, keepdims=True)
                grad_q = jnp.zeros((HEAD_DIM, CHUNK), jnp.float32)
                for side in range(2):
                    k = sides[side][h, 1]
                    s = dot_over(k, q, 0, 0) * (SCALE * LOG2E)
                    if side != own:
                        s = s + far
                    probs = jnp.exp2(s - lse)
                    grad_probs = dot_over(sides[side][h, 2], grad, 0, 0)
                    grad_scores = (probs * (grad_probs - delta)).astype(jnp.bfloat16)
                    grad_q = grad_q + dot_over(k, grad_scores, 1, 0)
                    grad_k = dot_over(q, grad_scores, 1, 1)
                    grad_v = dot_over(grad, probs.astype(jnp.bfloat16), 1, 1)
                    if first:
                        acc_ref[side, 0] = grad_k
                        acc_ref[side, 1] = grad_v
                    else:
                        acc_ref[side, 0] += grad_k
                        acc_ref[side, 1] += grad_v
                first = False
                res_ref[own, start // CHUNK, h, 0] = (grad_q * SCALE).astype(jnp.bfloat16)
        for side in range(2):
            for part in range(2):
                span = slice(part * rows, (part + 1) * rows)
                res_ref[side, part, h, 1] = (acc_ref[side, 0, :, span] * SCALE).astype(
                    jnp.bfloat16
                )
                res_ref[side, part, h, 2] = acc_ref[side, 1, :, span].astype(jnp.bfloat16)
        for to in range(2):
            back(h, to, core).start()
        for side in range(2):
            swap_back(h, side).start()
        pl.when(h > 0)(lambda: pass_back(h - 1))
        return carry

    lax.fori_loop(0, QUARTER, one_grad, 0)
    pass_back(QUARTER - 1)
    outs = (gq_ref, gk_ref, gv_ref)

    def settle(h, carry):
        for side in range(2):
            swap_back(h, side).wait_recv()

        @pl.when(has_source)
        def _():
            for slot in range(2):
                far_back(h, slot).wait_recv()

        for kind in range(3):
            for its_core, own, alone in (
                (core, res_ref[0, 0, h, kind], res_ref[1, 0, h, kind]),
                (1 - core, swap_back_ref[0, h, kind], swap_back_ref[1, h, kind]),
            ):
                came = chosen(
                    beside, back_ref[its_core, h, kind], far_back_ref[its_core, h, kind]
                )
                other = chosen(paired, came, alone)
                outs[kind][0, its_core, h] = chosen(late, other, own)
                outs[kind][1, its_core, h] = chosen(late, own, other)
        return carry

    lax.fori_loop(0, QUARTER, settle, 0)
    for kind in range(4):
        swap(kind).wait_send()
    for to in range(2):
        near_up(to, core).wait_send()
        pl.when(has_target)(lambda to=to: relay_up(to).wait_send())

    def drain(h, carry):
        for to in range(2):
            near(h, to, core).wait_send()
            back(h, to, core).wait_send()
            swap_back(h, to).wait_send()

        @pl.when(has_target)
        def _():
            for slot in range(2):
                relay(h, slot).wait_send()
                far_back(h, slot).wait_send()

        return carry

    lax.fori_loop(0, QUARTER, drain, 0)


SMEM = pl.BlockSpec(memory_space=pltpu.SMEM)
VMEM = pl.BlockSpec(memory_space=pltpu.VMEM)


def on_device(queries, keys, values, upstream, lengths, modality, pairs, texts, modality_bias):
    rows = queries.shape[0]
    devices = lax.axis_size("ctx")
    count = lengths.shape[0]
    assert rows * 2 == BLOCK
    xs = [x.T.reshape(2, 2, QUARTER, HEAD_DIM, rows) for x in (queries, keys, values, upstream)]
    text = texts.reshape(count, 2, 2, QUARTER, HEAD_DIM).transpose(0, 2, 1, 3, 4)
    text = jnp.pad(text.reshape(count, HEADS, HEAD_DIM), ((0, 0), (0, 0), (0, 128 - HEAD_DIM)))
    bf16, f32 = jnp.bfloat16, jnp.float32
    tile = (HEAD_DIM, rows)
    wide = (HEAD_DIM, BLOCK)
    dma = pltpu.SemaphoreType.DMA
    shaped = jax.ShapeDtypeStruct((2, 2, QUARTER) + tile, bf16)
    gq, gk, gv, loss = pl.pallas_call(
        step_kernel,
        in_specs=[SMEM] * 4 + [VMEM] * 5,
        out_specs=[VMEM] * 4,
        out_shape=[shaped, shaped, shaped, jax.ShapeDtypeStruct((8, 128), f32)],
        scratch_shapes=[
            pltpu.VMEM((2, QUARTER, 3) + tile, bf16),
            pltpu.VMEM((2, QUARTER) + tile, bf16),
            pltpu.VMEM((2, QUARTER, 3) + tile, bf16),
            pltpu.VMEM((2, QUARTER) + tile, bf16),
            pltpu.VMEM((2, QUARTER, 3) + tile, bf16),
            pltpu.VMEM((2, QUARTER) + tile, bf16),
            pltpu.VMEM((4, 2, QUARTER) + tile, bf16),
            pltpu.VMEM((QUARTER, 4) + wide, bf16),
            pltpu.VMEM((QUARTER, 4) + wide, bf16),
            pltpu.VMEM((2, QUARTER) + wide, bf16),
            pltpu.VMEM((2, QUARTER, 1, BLOCK), f32),
            pltpu.VMEM((8, 128), f32),
            pltpu.VMEM((devices, 8, 128), f32),
            pltpu.VMEM((2, QUARTER, HEAD_DIM, 1), f32),
            pltpu.VMEM((2, 2, QUARTER, 3) + tile, bf16),
            pltpu.VMEM((2, QUARTER, 3) + tile, bf16),
            pltpu.VMEM((2, QUARTER, 3) + tile, bf16),
            pltpu.VMEM((2, QUARTER, 3) + tile, bf16),
            pltpu.VMEM((2, 2) + wide, f32),
            dma((2, 4)),
            dma((2, 2, QUARTER + 1)),
            dma((2, 2, QUARTER + 1)),
            dma((2, devices)),
            dma((2, 2, QUARTER)),
            dma((2, 2, QUARTER)),
            dma((2, 2, QUARTER)),
        ],
        compiler_params=pltpu.CompilerParams(
            vmem_limit_bytes=48 * 2**20, collective_id=0, has_side_effects=True
        ),
        name="scene_step",
    )(lengths, modality, pairs, modality_bias, *xs, text)
    back = [g.reshape(HEADS * HEAD_DIM, rows).T for g in (gq, gk, gv)]
    return back[0], back[1], back[2], loss[0, :count]


def solution(mesh):
    tokens = P(("groups", "ctx"), None)
    in_specs = (
        tokens, tokens, tokens, tokens,
        P("groups"), P("groups"), P("groups"), P("groups", None), P(),
    )
    out_specs = (tokens, tokens, tokens, P("groups"))
    return jax.shard_map(
        on_device, mesh=mesh, in_specs=in_specs, out_specs=out_specs, check_vma=False
    )
```

```python
import jax
import jax.numpy as jnp
from jax import lax
from jax.experimental import pallas as pl
from jax.experimental.pallas import tpu as pltpu
from jax.sharding import PartitionSpec as P

HEADS = 16
HEAD_DIM = 72
BLOCK = 512
QUARTER = 4
CHUNK = 256
TEMPER = 10.0
LOSS_SCALE = 65536.0
EPSILON = 1e-06
SCALE = HEAD_DIM ** (-0.5)
LOG2E = 1.4426950408889634
FAR = -1e30


def dot_over(x, y, dim_x, dim_y):
    return lax.dot_general(
        x, y, (((dim_x,), (dim_y,)), ((), ())), preferred_element_type=jnp.float32
    )


def chosen(flag, x, y):
    return jnp.where(flag, x.astype(jnp.float32), y.astype(jnp.float32)).astype(jnp.bfloat16)


def step_kernel(
    lengths_ref, modality_ref, pairs_ref, bias_ref,
    q_ref, k_ref, v_ref, u_ref, texts_ref,
    gq_ref, gk_ref, gv_ref, loss_ref,
    place_ref, send_ref, sendu_ref, near_ref, nearu_ref, relay_ref, relayu_ref, swap_ref,
    a_ref, b_ref, att_ref, lse_ref, note_ref, pools_ref, extra_ref,
    res_ref, back_ref, far_back_ref, swap_back_ref, acc_ref,
    swap_sems, near_sems, relay_sems, note_sems, back_sems, far_back_sems, swap_back_sems,
):
    devices = lax.axis_size("ctx")
    blocks = devices // 2
    count = texts_ref.shape[0]
    rows = BLOCK // 2
    me = lax.axis_index("ctx")
    core = me % 2
    block = me // 2
    odd = block % 2
    mate = me + 1 - 2 * core
    across = (block + 1 - 2 * odd) * 2
    target = me + 4 - 8 * odd
    source = me - 4 + 8 * odd
    has_target = (target >= 0) & (target < devices)
    has_source = (source >= 0) & (source < devices)

    barrier = pltpu.get_barrier_semaphore()

    def peer(step):
        return (me + step) % devices

    def greet_one(step, carry):
        pl.semaphore_signal(
            barrier, inc=1, device_id={"ctx": peer(step)}, device_id_type=pl.DeviceIdType.MESH
        )
        return carry

    lax.fori_loop(1, devices, greet_one, 0)

    def place_of(at):
        scene, start, length, end = 0, 0, 0, 0
        for s in range(count):
            begin = end
            end = end + lengths_ref[s]
            here = (at >= begin) & (at < end)
            scene = jnp.where(here, s, scene)
            start = jnp.where(here, begin, start)
            length = jnp.where(here, lengths_ref[s], length)
        return scene, at - start, length

    scene, second, length = place_of(block)
    paired = length == 2
    late = second == 1
    beside = (block + 1 - 2 * second) == (block + 1 - 2 * odd)
    far = jnp.where(paired, 0.0, FAR).astype(jnp.float32)
    inputs = (q_ref, k_ref, v_ref, u_ref)

    def remote(src, dst, send_sem, recv_sem, device):
        return pltpu.make_async_remote_copy(
            src_ref=src,
            dst_ref=dst,
            send_sem=send_sem,
            recv_sem=recv_sem,
            device_id={"ctx": device},
            device_id_type=pl.DeviceIdType.MESH,
        )

    def swap(kind):
        return remote(
            inputs[kind].at[:, 1 - core], swap_ref.at[kind],
            swap_sems.at[0, kind], swap_sems.at[1, kind], mate,
        )

    def near(h, to, slot):
        return remote(
            send_ref.at[to, h], near_ref.at[slot, h],
            near_sems.at[0, to, h], near_sems.at[1, slot, h], across + to,
        )

    def near_up(to, slot):
        return remote(
            sendu_ref.at[to], nearu_ref.at[slot],
            near_sems.at[0, to, QUARTER], near_sems.at[1, slot, QUARTER], across + to,
        )

    def relay(h, slot):
        return remote(
            near_ref.at[slot, h], relay_ref.at[slot, h],
            relay_sems.at[0, slot, h], relay_sems.at[1, slot, h], target,
        )

    def relay_up(slot):
        return remote(
            nearu_ref.at[slot], relayu_ref.at[slot],
            relay_sems.at[0, slot, QUARTER], relay_sems.at[1, slot, QUARTER], target,
        )

    def back(h, to, slot):
        return remote(
            res_ref.at[1, to, h], back_ref.at[slot, h],
            back_sems.at[0, to, h], back_sems.at[1, slot, h], across + to,
        )

    def far_back(h, slot):
        return remote(
            back_ref.at[slot, h], far_back_ref.at[slot, h],
            far_back_sems.at[0, slot, h], far_back_sems.at[1, slot, h], target,
        )

    def swap_back(h, side):
        return remote(
            res_ref.at[side, 1, h], swap_back_ref.at[side, h],
            swap_back_sems.at[0, side, h], swap_back_sems.at[1, side, h], mate,
        )

    @pl.when(jnp.logical_not(has_source))
    def _():
        relay_ref[...] = jnp.zeros_like(relay_ref)
        relayu_ref[...] = jnp.zeros_like(relayu_ref)
        far_back_ref[...] = jnp.zeros_like(far_back_ref)

    def fill(h, carry):
        for to in range(2):
            for kind in range(3):
                send_ref[to, h, kind] = chosen(
                    late, inputs[kind][0, to, h], inputs[kind][1, to, h]
                )
            sendu_ref[to, h] = chosen(late, u_ref[0, to, h], u_ref[1, to, h])
        return carry

    lax.fori_loop(0, QUARTER, fill, 0)
    pl.semaphore_wait(barrier, devices - 1)
    for h in range(2):
        for to in range(2):
            near(h, to, core).start()
    for kind in range(4):
        swap(kind).start()

    def pass_on(h):
        for slot in range(2):
            near(h, slot, slot).wait_recv()

        @pl.when(h < QUARTER - 2)
        def _():
            for to in range(2):
                near(h + 2, to, core).start()

        @pl.when(h == QUARTER - 2)
        def _():
            for to in range(2):
                near_up(to, core).start()

        for slot in range(2):
            pl.when(has_target)(lambda slot=slot: relay(h, slot).start())

    place_ref[...] = jnp.zeros_like(place_ref)
    for row in range(HEADS):
        half, its_core, h = row // 8, (row // 4) % 2, row % 4
        piece = texts_ref[:, row * HEAD_DIM : (row + 1) * HEAD_DIM]
        place_ref[:, its_core * 8 + half * 4 + h, :HEAD_DIM] = piece
    for kind in range(4):
        swap(kind).wait_recv()
    lax.fori_loop(0, 1, lambda h, carry: (pass_on(h), carry)[1], 0)
    lane = lax.broadcasted_iota(jnp.int32, (HEAD_DIM, 128), 1)
    sides = (a_ref, b_ref)

    def own_tiles(h, kind, near_pair, relay_pair):
        x = inputs[kind]
        low, high = x[0, core, h], x[1, core, h]
        low_far, high_far = swap_ref[kind, 0, h], swap_ref[kind, 1, h]
        a_ref[h, kind, :, :rows] = chosen(late, high, low)
        a_ref[h, kind, :, rows:] = chosen(late, high_far, low_far)
        for slot, alone in ((0, high), (1, high_far)):
            b_ref[h, kind, :, slot * rows : (slot + 1) * rows] = chosen(
                paired, chosen(beside, near_pair[slot], relay_pair[slot]), alone
            )

    def one_head(h, gathered):
        pl.when(h < QUARTER - 1)(lambda: pass_on(h + 1))

        @pl.when(has_source)
        def _():
            for slot in range(2):
                relay(h, slot).wait_recv()

        for kind in range(3):
            own_tiles(
                h, kind,
                [near_ref[slot, h, kind] for slot in range(2)],
                [relay_ref[slot, h, kind] for slot in range(2)],
            )
        for own in range(2):
            pool = jnp.zeros((HEAD_DIM, 1), jnp.float32)
            for start in range(0, BLOCK, CHUNK):
                q = sides[own][h, 0, :, start : start + CHUNK]
                scores = []
                for side in range(2):
                    s = dot_over(sides[side][h, 1], q, 0, 0) * (SCALE * LOG2E)
                    scores.append(s if side == own else s + far)
                top = jnp.maximum(
                    jnp.max(scores[0], axis=0, keepdims=True),
                    jnp.max(scores[1], axis=0, keepdims=True),
                )
                parts = [jnp.exp2(s - top) for s in scores]
                total = jnp.sum(parts[0], axis=0, keepdims=True) + jnp.sum(
                    parts[1], axis=0, keepdims=True
                )
                scale = 1.0 / total
                att = jnp.zeros((HEAD_DIM, CHUNK), jnp.float32)
                for side in range(2):
                    probs = (parts[side] * scale).astype(jnp.bfloat16)
                    att = att + dot_over(sides[side][h, 2], probs, 1, 0)
                att = att.astype(jnp.bfloat16)
                att_ref[own, h, :, start : start + CHUNK] = att
                lse_ref[own, h, :, start : start + CHUNK] = top + jnp.log2(total)
                pool = pool + jnp.sum(att.astype(jnp.float32), axis=1, keepdims=True)
            gathered = jnp.where(lane == own * QUARTER + h, pool, gathered)
        return gathered

    pool = lax.fori_loop(0, QUARTER, one_head, jnp.zeros((HEAD_DIM, 128), jnp.float32))
    pool = jnp.concatenate([pool, jnp.zeros((128 - HEAD_DIM, 128), jnp.float32)], axis=0)
    note_ref[...] = pool.T[: 2 * QUARTER]

    def note(step, slot):
        return remote(
            note_ref, pools_ref.at[slot], note_sems.at[0, step], note_sems.at[1, step], peer(step)
        )

    def send_note(step, carry):
        note(step, me).start()
        return carry

    lax.fori_loop(1, devices, send_note, 0)
    pools_ref[me] = note_ref[...]
    for slot in range(2):
        near_up(slot, slot).wait_recv()
    for slot in range(2):
        pl.when(has_target)(lambda slot=slot: relay_up(slot).start())

    text = place_ref[...]

    def total_of(x):
        return jnp.sum(jnp.sum(x, axis=2, keepdims=True), axis=1, keepdims=True)

    text_unit = text / jnp.sqrt(total_of(text * text) + EPSILON)
    which = lax.broadcasted_iota(jnp.int32, (count, 1, 1), 0)
    which_full = lax.broadcasted_iota(jnp.int32, (count, 16, 128), 0)
    row_half = lax.broadcasted_iota(jnp.int32, (8, 128), 0) // QUARTER

    def wait_note(step, carry):
        done = note(step, (me + devices - step) % devices)
        done.wait_recv()
        done.wait_send()
        return carry

    lax.fori_loop(1, devices, wait_note, 0)

    def add_block(at, sums):
        its_scene, its_second, its_length = place_of(at)
        pieces = []
        for its_core in range(2):
            x = pools_ref[2 * at + its_core]
            both = x + jnp.concatenate([x[QUARTER:], x[:QUARTER]], axis=0)
            both = jnp.where(row_half == its_second, both, 0.0)
            pieces.append(jnp.where(its_length == 2, both, x))
        piece = jnp.concatenate(pieces, axis=0)
        return sums + jnp.where(which_full == its_scene, piece[None], 0.0)

    sums = lax.fori_loop(0, blocks, add_block, jnp.zeros((count, 16, 128), jnp.float32))
    sizes = jnp.zeros((count, 1, 1), jnp.float32)
    for s in range(count):
        sizes = jnp.where(which == s, (lengths_ref[s] * BLOCK).astype(jnp.float32), sizes)
    pooled = sums / sizes
    norm = jnp.sqrt(total_of(pooled * pooled) + EPSILON)
    unit = pooled / norm
    loss = jnp.zeros((8, 128), jnp.float32)
    loss_lane = lax.broadcasted_iota(jnp.int32, (8, 128), 1)
    grad_logits = jnp.zeros((count, 1, 1), jnp.float32)
    for i in range(count):
        bias = jnp.where(modality_ref[i] == 0, bias_ref[0], bias_ref[1])
        logits = TEMPER * total_of(text_unit * unit[i : i + 1]) + bias
        label = jnp.where(which == pairs_ref[i], 1.0, -1.0)
        margin = label * logits
        plus = jnp.maximum(-margin, 0.0) + jnp.log1p(jnp.exp(-jnp.abs(margin)))
        loss = jnp.where(loss_lane == i, jnp.sum(plus, axis=0), loss)
        slope = -label / (1.0 + jnp.exp(margin)) * (LOSS_SCALE / count)
        grad_logits = jnp.where(scene == i, slope, grad_logits)
    loss_ref[...] = loss
    grad_unit = TEMPER * jnp.sum(grad_logits * text_unit, axis=0, keepdims=True)
    mine = which == scene
    my_unit = jnp.sum(jnp.where(which_full == scene, unit, 0.0), axis=0, keepdims=True)
    my_norm = jnp.sum(jnp.where(mine, norm, 0.0), axis=0, keepdims=True)
    my_size = (length * BLOCK).astype(jnp.float32)
    grad_pooled = (grad_unit - my_unit * total_of(my_unit * grad_unit)) / my_norm
    per_token = (grad_pooled / my_size)[0]
    per_core = jnp.where(core == 0, per_token[:8], per_token[8:])
    columns = jnp.concatenate([per_core, jnp.zeros((120, 128), jnp.float32)], axis=0).T
    for h in range(QUARTER):
        low = columns[:HEAD_DIM, h : h + 1]
        high = columns[:HEAD_DIM, QUARTER + h : QUARTER + h + 1]
        own = jnp.where(late, high, low)
        extra_ref[0, h] = own
        extra_ref[1, h] = jnp.where(paired, own, high)

    @pl.when(has_source)
    def _():
        for slot in range(2):
            relay_up(slot).wait_recv()

    def pass_back(h):
        for slot in range(2):
            back(h, slot, slot).wait_recv()
        for slot in range(2):
            pl.when(has_target)(lambda slot=slot: far_back(h, slot).start())

    def one_grad(h, carry):
        own_tiles(
            h, 3,
            [nearu_ref[slot, h] for slot in range(2)],
            [relayu_ref[slot, h] for slot in range(2)],
        )
        first = True
        for own in range(2):
            for start in range(0, BLOCK, CHUNK):
                span = slice(start, start + CHUNK)
                q = sides[own][h, 0, :, span]
                up = sides[own][h, 3, :, span].astype(jnp.float32)
                grad = (up + extra_ref[own, h]).astype(jnp.bfloat16)
                att = att_ref[own, h, :, span].astype(jnp.float32)
                lse = lse_ref[own, h, :, span]
                delta = jnp.sum(grad.astype(jnp.float32) * att, axis=0, keepdims=True)
                grad_q = jnp.zeros((HEAD_DIM, CHUNK), jnp.float32)
                for side in range(2):
                    k = sides[side][h, 1]
                    s = dot_over(k, q, 0, 0) * (SCALE * LOG2E)
                    if side != own:
                        s = s + far
                    probs = jnp.exp2(s - lse)
                    grad_probs = dot_over(sides[side][h, 2], grad, 0, 0)
                    grad_scores = (probs * (grad_probs - delta)).astype(jnp.bfloat16)
                    grad_q = grad_q + dot_over(k, grad_scores, 1, 0)
                    grad_k = dot_over(q, grad_scores, 1, 1)
                    grad_v = dot_over(grad, probs.astype(jnp.bfloat16), 1, 1)
                    if first:
                        acc_ref[side, 0] = grad_k
                        acc_ref[side, 1] = grad_v
                    else:
                        acc_ref[side, 0] += grad_k
                        acc_ref[side, 1] += grad_v
                first = False
                res_ref[own, start // CHUNK, h, 0] = (grad_q * SCALE).astype(jnp.bfloat16)
        for side in range(2):
            for part in range(2):
                span = slice(part * rows, (part + 1) * rows)
                res_ref[side, part, h, 1] = (acc_ref[side, 0, :, span] * SCALE).astype(
                    jnp.bfloat16
                )
                res_ref[side, part, h, 2] = acc_ref[side, 1, :, span].astype(jnp.bfloat16)
        for to in range(2):
            back(h, to, core).start()
        for side in range(2):
            swap_back(h, side).start()
        pl.when(h > 0)(lambda: pass_back(h - 1))
        return carry

    lax.fori_loop(0, QUARTER, one_grad, 0)
    pass_back(QUARTER - 1)
    outs = (gq_ref, gk_ref, gv_ref)

    def settle(h, carry):
        for side in range(2):
            swap_back(h, side).wait_recv()

        @pl.when(has_source)
        def _():
            for slot in range(2):
                far_back(h, slot).wait_recv()

        for kind in range(3):
            for its_core, own, alone in (
                (core, res_ref[0, 0, h, kind], res_ref[1, 0, h, kind]),
                (1 - core, swap_back_ref[0, h, kind], swap_back_ref[1, h, kind]),
            ):
                came = chosen(
                    beside, back_ref[its_core, h, kind], far_back_ref[its_core, h, kind]
                )
                other = chosen(paired, came, alone)
                outs[kind][0, its_core, h] = chosen(late, other, own)
                outs[kind][1, its_core, h] = chosen(late, own, other)
        return carry

    lax.fori_loop(0, QUARTER, settle, 0)
    for kind in range(4):
        swap(kind).wait_send()
    for to in range(2):
        near_up(to, core).wait_send()
        pl.when(has_target)(lambda to=to: relay_up(to).wait_send())

    def drain(h, carry):
        for to in range(2):
            near(h, to, core).wait_send()
            back(h, to, core).wait_send()
            swap_back(h, to).wait_send()

        @pl.when(has_target)
        def _():
            for slot in range(2):
                relay(h, slot).wait_send()
                far_back(h, slot).wait_send()

        return carry

    lax.fori_loop(0, QUARTER, drain, 0)


SMEM = pl.BlockSpec(memory_space=pltpu.SMEM)
VMEM = pl.BlockSpec(memory_space=pltpu.VMEM)


def on_device(queries, keys, values, upstream, lengths, modality, pairs, texts, modality_bias):
    rows = queries.shape[0]
    devices = lax.axis_size("ctx")
    count = lengths.shape[0]
    assert rows * 2 == BLOCK
    xs = [x.T.reshape(2, 2, QUARTER, HEAD_DIM, rows) for x in (queries, keys, values, upstream)]
    bf16, f32 = jnp.bfloat16, jnp.float32
    tile = (HEAD_DIM, rows)
    wide = (HEAD_DIM, BLOCK)
    dma = pltpu.SemaphoreType.DMA
    shaped = jax.ShapeDtypeStruct((2, 2, QUARTER) + tile, bf16)
    gq, gk, gv, loss = pl.pallas_call(
        step_kernel,
        in_specs=[SMEM] * 4 + [VMEM] * 5,
        out_specs=[VMEM] * 4,
        out_shape=[shaped, shaped, shaped, jax.ShapeDtypeStruct((8, 128), f32)],
        scratch_shapes=[
            pltpu.VMEM((count, HEADS, 128), f32),
            pltpu.VMEM((2, QUARTER, 3) + tile, bf16),
            pltpu.VMEM((2, QUARTER) + tile, bf16),
            pltpu.VMEM((2, QUARTER, 3) + tile, bf16),
            pltpu.VMEM((2, QUARTER) + tile, bf16),
            pltpu.VMEM((2, QUARTER, 3) + tile, bf16),
            pltpu.VMEM((2, QUARTER) + tile, bf16),
            pltpu.VMEM((4, 2, QUARTER) + tile, bf16),
            pltpu.VMEM((QUARTER, 4) + wide, bf16),
            pltpu.VMEM((QUARTER, 4) + wide, bf16),
            pltpu.VMEM((2, QUARTER) + wide, bf16),
            pltpu.VMEM((2, QUARTER, 1, BLOCK), f32),
            pltpu.VMEM((8, 128), f32),
            pltpu.VMEM((devices, 8, 128), f32),
            pltpu.VMEM((2, QUARTER, HEAD_DIM, 1), f32),
            pltpu.VMEM((2, 2, QUARTER, 3) + tile, bf16),
            pltpu.VMEM((2, QUARTER, 3) + tile, bf16),
            pltpu.VMEM((2, QUARTER, 3) + tile, bf16),
            pltpu.VMEM((2, QUARTER, 3) + tile, bf16),
            pltpu.VMEM((2, 2) + wide, f32),
            dma((2, 4)),
            dma((2, 2, QUARTER + 1)),
            dma((2, 2, QUARTER + 1)),
            dma((2, devices)),
            dma((2, 2, QUARTER)),
            dma((2, 2, QUARTER)),
            dma((2, 2, QUARTER)),
        ],
        compiler_params=pltpu.CompilerParams(
            vmem_limit_bytes=48 * 2**20, collective_id=0, has_side_effects=True
        ),
        name="scene_step",
    )(lengths, modality, pairs, modality_bias, *xs, texts)
    back = [g.reshape(HEADS * HEAD_DIM, rows).T for g in (gq, gk, gv)]
    return back[0], back[1], back[2], loss[0, :count]


def solution(mesh):
    tokens = P(("groups", "ctx"), None)
    in_specs = (
        tokens, tokens, tokens, tokens,
        P("groups"), P("groups"), P("groups"), P("groups", None), P(),
    )
    out_specs = (tokens, tokens, tokens, P("groups"))
    return jax.shard_map(
        on_device, mesh=mesh, in_specs=in_specs, out_specs=out_specs, check_vma=False
    )
```
